32 devices in a mesh: clip: 4 (over y, core), row: 2 (over x), src: 4 (over z).
Axes of the slice: x: 2, y: 2, z: 4, core: 2. Of those that a mesh axis runs over, the one named last changes fastest.
Arguments:
- mask_clip: bfloat16 [16384, 4096], P(('clip', 'row'), 'src'), parts along dimension 0, may hold values from -6 to 6
- source_shifts: int32 [16, 2], P('src'), may hold values from -64 to 64
- source_weights: int32 [16], P('src'), may hold values from 1 to 8
Outputs:
- intensity: float32 [4096, 1024], P(('clip', 'row', 'src')), parts along dimension 0
The draws below stay inside these ranges and needn't reach their ends.
There are 4 independent parts, one for each index of `clip`. The reference program is written for one: setup_inputs(seed, part) draws one part's arguments, and reference() takes and returns one part's arrays. A program takes and returns all parts, laid end to end along the dimension named above; an argument that names none is the same for every part. Nothing has to cross between parts.
All inputs are finite; a program needn't handle non-finite values.
Results may differ from the reference program's by a relative error of at most 0.0052.
Values may be sent and summed in bfloat16 or wider, within the bound.
A program may use at most 64 MiB of HBM per device.

```python
import math
import jax
import jax.numpy as jnp
from jax import lax

NM = 4096
P_SIZE = 256
NI = 1024
SOURCES = 16
N_ROW = 2
N_SRC = 4


def with_ends(values, rng, least, top_value):
    place = [jax.random.randint(jax.random.fold_in(rng, axis), (), 0, length) for axis, length in enumerate(values.shape)]
    longest = values.shape.index(max(values.shape))
    neighbour = place[:longest] + [(place[longest] + 1) % values.shape[longest]] + place[longest + 1:]
    return values.at[tuple(place)].set(least).at[tuple(neighbour)].set(top_value)


def shard_levels(stream_key, extent, shards, smallest, top_value):
    loudness, own = 1.0, jax.random.fold_in(stream_key, 6)
    for dim, blocks in shards:
        heights = jnp.exp(jax.random.uniform(jax.random.fold_in(own, dim), (blocks,), jnp.float32, smallest / len(shards), top_value / len(shards)))
        loudness = loudness * jnp.repeat(heights, extent[dim] // blocks).reshape([-1 if axis == dim else 1 for axis in range(len(extent))])
    return loudness


def centred(stream_key, shape, scale, limit, cuts=(), held_as=jnp.bfloat16):
    drawn = scale * jax.random.normal(stream_key, shape, jnp.float32)
    if cuts:
        drawn = drawn * shard_levels(stream_key, shape, cuts, -0.22, 0.18)
    return jnp.clip(drawn, -limit, limit).astype(held_as)


def setup_inputs(seed: int = 0, part: int = 0) -> dict:
    keys = jax.random.split(jax.random.key(seed), 4)
    part_splits = jax.random.split(jax.random.fold_in(keys[3], part), 4)
    return {
        "mask_clip": centred(part_splits[0], (NM, NM), 1.0, 6.0, ((0, 2), (1, 4))),
        "source_shifts": with_ends(jax.random.randint(keys[1], (SOURCES, 2), 0 - P_SIZE // 4, P_SIZE // 4 + 1), jax.random.fold_in(keys[1], 1), 0 - P_SIZE // 4, (P_SIZE // 4 + 1) - 1).astype(jnp.int32),
        "source_weights": with_ends(jax.random.randint(keys[2], (SOURCES,), 1, 9), jax.random.fold_in(keys[2], 1), 1, 8).astype(jnp.int32),
    }


def twiddles(positions, length, scaling):
    frequency = jnp.arange(P_SIZE, dtype=jnp.int32) - P_SIZE // 2
    product = jnp.mod(positions[:, None] * frequency[None, :], length)
    angles = product.astype(jnp.float32) * jnp.float32(2.0 * math.pi / length)
    return (jnp.cos(angles) * jnp.float32(scaling), jnp.sin(angles) * jnp.float32(scaling))

def tile_spectrum(mask_tile, row_first, col_first):
    row_index = row_first + jnp.arange(mask_tile.shape[0], dtype=jnp.int32)
    col_index = col_first + jnp.arange(mask_tile.shape[1], dtype=jnp.int32)
    col_cos, col_sin = twiddles(col_index, NM, 1.0 / math.sqrt(NM))
    col_table = jnp.concatenate([col_cos, -col_sin], 1).astype(jnp.bfloat16)
    half_way = jnp.dot(mask_tile, col_table, preferred_element_type=jnp.float32).astype(jnp.bfloat16)
    row_cos, row_sin = twiddles(row_index, NM, 1.0 / math.sqrt(NM))
    row_table = jnp.concatenate([row_cos, row_sin], 1).T.astype(jnp.bfloat16)
    blocks = jnp.dot(row_table, half_way, preferred_element_type=jnp.float32)
    real_part = blocks[:P_SIZE, :P_SIZE] + blocks[P_SIZE:, P_SIZE:]
    imag_part = blocks[:P_SIZE, P_SIZE:] - blocks[P_SIZE:, :P_SIZE]
    return jnp.stack([real_part, imag_part])

def build_left(image_rows):
    row_cos, row_sin = twiddles(image_rows, NI, 1.0 / math.sqrt(P_SIZE))
    return jnp.concatenate([row_cos, row_sin], 0).astype(jnp.bfloat16)

def build_right():
    col_cos, col_sin = twiddles(jnp.arange(NI, dtype=jnp.int32), NI, 1.0 / math.sqrt(P_SIZE))
    upper = jnp.concatenate([col_cos.T, col_sin.T], 1)
    lower = jnp.concatenate([-col_sin.T, col_cos.T], 1)
    return jnp.concatenate([upper, lower], 0).astype(jnp.bfloat16)

def source_image(spectrum, shift_pair, weight, left_table, right_table):
    frequency = jnp.arange(P_SIZE, dtype=jnp.int32) - P_SIZE // 2
    along_rows = frequency + shift_pair[0]
    along_cols = frequency + shift_pair[1]
    radius = P_SIZE // 4
    inside = along_rows[:, None] * along_rows[:, None] + along_cols[None, :] * along_cols[None, :] <= radius * radius
    pupil_mask = inside.astype(jnp.bfloat16)
    passed = jnp.concatenate([spectrum[0] * pupil_mask, spectrum[1] * pupil_mask], 1)
    blocks = jnp.dot(left_table, passed, preferred_element_type=jnp.float32)
    row_count = left_table.shape[0] // 2
    k_real = blocks[:row_count, :P_SIZE] - blocks[row_count:, P_SIZE:]
    k_imag = blocks[:row_count, P_SIZE:] + blocks[row_count:, :P_SIZE]
    partial_value = jnp.concatenate([k_real, k_imag], 1).astype(jnp.bfloat16)
    field_pair = jnp.dot(partial_value, right_table, preferred_element_type=jnp.float32)
    field_real = field_pair[:, :NI]
    field_imag = field_pair[:, NI:]
    return weight.astype(jnp.float32) * (field_real * field_real + field_imag * field_imag)

def reference(mask_clip, source_shifts, source_weights):
    strip_rows = NM // N_ROW
    strip_cols = NM // N_SRC
    running_sum = jnp.zeros((2, P_SIZE, P_SIZE), jnp.float32)
    for strip_row in range(N_ROW):
        for strip_col in range(N_SRC):
            mask_tile = mask_clip[strip_row * strip_rows:(strip_row + 1) * strip_rows, strip_col * strip_cols:(strip_col + 1) * strip_cols]
            running_sum = running_sum + tile_spectrum(mask_tile, strip_row * strip_rows, strip_col * strip_cols)
    spectrum = running_sum.astype(jnp.bfloat16)
    left_table = build_left(jnp.arange(NI, dtype=jnp.int32))
    right_table = build_right()

    def add_source(running, source_item):
        shift_pair, weight = source_item
        return (running + source_image(spectrum, shift_pair, weight, left_table, right_table), None)
    summed, _ = lax.scan(add_source, jnp.zeros((NI, NI), jnp.float32), (source_shifts, source_weights))
    return summed / jnp.float32(SOURCES)
```

```python
import functools
import math

import jax
import jax.numpy as jnp
import ml_dtypes
import numpy as np
from jax import lax
from jax.experimental import pallas as pl
from jax.experimental.pallas import tpu as pltpu
from jax.sharding import PartitionSpec as P

P_SIZE = 256
NI = 1024
COARSE = 512
MESH = pl.DeviceIdType.MESH
BF16 = ml_dtypes.bfloat16


def twiddles(positions, length, scaling):
    frequency = np.arange(P_SIZE) - P_SIZE // 2
    angles = np.mod(positions[:, None] * frequency[None, :], length) * (2.0 * math.pi / length)
    return np.cos(angles) * scaling, np.sin(angles) * scaling


@functools.lru_cache(maxsize=None)
def forward_table(length):
    cos, sin = twiddles(np.arange(length), length, 1.0 / math.sqrt(length))
    return np.concatenate([cos, sin], 1).astype(np.float32).astype(BF16)


@functools.lru_cache(maxsize=None)
def inverse_tables(row_blocks):
    cos, sin = twiddles(np.arange(NI), NI, 1.0 / math.sqrt(P_SIZE))
    cols = np.concatenate([cos, sin], 1)[:: NI // COARSE]
    block = NI // row_blocks
    rows = np.stack(
        [
            np.block([[c.T, s.T], [-s.T, c.T]])
            for c, s in zip(cos.reshape(-1, block, P_SIZE), sin.reshape(-1, block, P_SIZE))
        ]
    )
    band = P_SIZE // 2
    u = np.arange(-COARSE, COARSE + 1)
    ramp = np.clip((np.abs(u) - band) / (COARSE - 2 * band), 0.0, 1.0)
    gain = 0.5 + 0.5 * np.cos(math.pi * ramp)
    offset = np.arange(NI)
    kernel = (gain[None, :] * np.cos(2 * math.pi * offset[:, None] * u[None, :] / NI)).sum(1) / COARSE
    step = NI // COARSE
    spread = kernel[np.mod(np.arange(NI)[None, :] - step * np.arange(COARSE)[:, None], NI)]
    high = spread.astype(np.float32).astype(BF16)
    low = (spread - high.astype(np.float64)).astype(np.float32).astype(BF16)
    as_bf16 = lambda x: x.astype(np.float32).astype(BF16)
    return as_bf16(rows), as_bf16(cols), high, low


def spectrum_kernel(
    n_row, n_src, chunks,
    mask_hbm, col_hbm, row_hbm, own_ref,
    spec_ref, points_ref,
    mask, col, row, half, part, send, arrived,
    load_sem, rs_send, rs_recv, ag_send, ag_recv, pt_send, pt_recv,
):
    n = n_row * n_src
    row_id, src_id = lax.axis_index("row"), lax.axis_index("src")
    me = row_id * n_src + src_id
    rows, cols = mask.shape
    piece = rows // chunks
    per = P_SIZE // n

    loads = [
        pltpu.make_async_copy(
            col_hbm.at[pl.ds(pl.multiple_of(src_id * cols, cols), cols)], col, load_sem.at[0]
        )
    ]
    for i in range(chunks):
        loads.append(
            pltpu.make_async_copy(
                mask_hbm.at[pl.ds(i * piece, piece)], mask.at[pl.ds(i * piece, piece)],
                load_sem.at[1 + i],
            )
        )
    loads.append(
        pltpu.make_async_copy(
            row_hbm.at[:, pl.ds(pl.multiple_of(row_id * rows, rows), rows)], row,
            load_sem.at[1 + chunks],
        )
    )
    for load in loads:
        load.start()

    def partner(k):
        other = lax.rem(me + k, n)
        return other, {"row": other // n_src, "src": lax.rem(other, n_src)}

    barrier = pltpu.get_barrier_semaphore()
    for k in range(1, n):
        pl.semaphore_signal(barrier, inc=1, device_id=partner(k)[1], device_id_type=MESH)

    loads[0].wait()
    for i in range(chunks):
        loads[1 + i].wait()
        half[pl.ds(i * piece, piece)] = jnp.dot(
            mask[pl.ds(i * piece, piece)], col[...], preferred_element_type=jnp.float32
        ).astype(jnp.bfloat16)
    loads[-1].wait()
    blocks = jnp.dot(row[...], half[...], preferred_element_type=jnp.float32)
    p = P_SIZE
    part[:, :p] = blocks[:p, :p] - blocks[p:, p:]
    part[:, p:] = -blocks[:p, p:] - blocks[p:, :p]
    send[...] = part[...].astype(jnp.bfloat16)

    pl.semaphore_wait(barrier, n - 1)
    outgoing = []
    for k in range(1, n):
        other, where = partner(k)
        copy = pltpu.make_async_remote_copy(
            src_ref=send.at[pl.ds(pl.multiple_of(other * per, per), per)],
            dst_ref=arrived.at[k],
            send_sem=rs_send.at[k], recv_sem=rs_recv.at[k],
            device_id=where, device_id_type=MESH,
        )
        copy.start()
        outgoing.append(copy)
    point_copies = []
    for k in range(1, n_src):
        copy = pltpu.make_async_remote_copy(
            src_ref=own_ref, dst_ref=points_ref.at[src_id],
            send_sem=pt_send.at[k], recv_sem=pt_recv.at[k],
            device_id={"src": lax.rem(src_id + k, n_src)}, device_id_type=MESH,
        )
        copy.start()
        point_copies.append(copy)
    points_ref[src_id] = own_ref[...]

    mine = pl.ds(pl.multiple_of(me * per, per), per)
    total = part[mine]
    for k, copy in enumerate(outgoing, 1):
        copy.wait_recv()
        total = total + arrived[k].astype(jnp.float32)
    spec_ref[mine] = total.astype(jnp.bfloat16)
    gathered = []
    for k in range(1, n):
        copy = pltpu.make_async_remote_copy(
            src_ref=spec_ref.at[mine], dst_ref=spec_ref.at[mine],
            send_sem=ag_send.at[k], recv_sem=ag_recv.at[k],
            device_id=partner(k)[1], device_id_type=MESH,
        )
        copy.start()
        gathered.append(copy)
    for copy in point_copies + gathered:
        copy.wait_recv()
    for copy in outgoing + point_copies + gathered:
        copy.wait_send()


def image_kernel(spec_ref, points, rows_hbm, col_ref, high_ref, low_ref, out_ref, rows, turned, halves, total, sem):
    n_src = lax.axis_size("src")
    me = lax.axis_index("row") * n_src + lax.axis_index("src")
    load = pltpu.make_async_copy(rows_hbm.at[me], rows, sem.at[0])
    load.start()
    p = P_SIZE
    block = out_ref.shape[0]
    per = points.shape[1]
    sources = points.shape[0] * per
    turned[:, :p] = spec_ref[:, :p].astype(jnp.float32).T.astype(jnp.bfloat16)
    turned[:, p:] = spec_ref[:, p:].astype(jnp.float32).T.astype(jnp.bfloat16)
    along_rows = lax.broadcasted_iota(jnp.int32, (p, p), 1) - p // 2
    along_cols = lax.broadcasted_iota(jnp.int32, (p, p), 0) - p // 2
    radius = p // 4
    load.wait()

    def first(s, carry):
        down = along_rows + points[s // per, lax.rem(s, per), 0]
        across = along_cols + points[s // per, lax.rem(s, per), 1]
        inside = down * down + across * across <= radius * radius
        pupil = jnp.where(inside, 1.0, 0.0).astype(jnp.bfloat16)
        passed = jnp.concatenate([turned[:, :p] * pupil, turned[:, p:] * pupil], 1)
        k = jnp.dot(passed, rows[...], preferred_element_type=jnp.float32).astype(jnp.bfloat16)
        halves[s, :p] = k
        halves[s, p:, :block] = -k[:, block:]
        halves[s, p:, block:] = k[:, :block]
        return carry

    lax.fori_loop(0, sources, first, 0, unroll=2)
    total[...] = jnp.zeros_like(total)

    def second(s, carry):
        weight = points[s // per, lax.rem(s, per), 2].astype(jnp.float32) * (1.0 / sources)
        e = jnp.dot(col_ref[...], halves[s], preferred_element_type=jnp.float32)
        total[...] += weight * (e[:, :block] * e[:, :block] + e[:, block:] * e[:, block:])
        return carry

    lax.fori_loop(0, sources, second, 0, unroll=2)
    summed = total[...].T
    top = summed.astype(jnp.bfloat16)
    rest = (summed - top.astype(jnp.float32)).astype(jnp.bfloat16)
    out_ref[...] = (
        jnp.dot(top, high_ref[...], preferred_element_type=jnp.float32)
        + jnp.dot(rest, high_ref[...], preferred_element_type=jnp.float32)
        + jnp.dot(top, low_ref[...], preferred_element_type=jnp.float32)
    )


def body(n_row, n_src, mask_clip, source_shifts, source_weights):
    n = n_row * n_src
    rows, cols = mask_clip.shape
    per = P_SIZE // n
    own = jnp.concatenate([source_shifts, source_weights[:, None]], 1)
    chunks = 4
    vmem = pl.BlockSpec(memory_space=pltpu.VMEM)
    anywhere = pl.BlockSpec(memory_space=pl.ANY)
    spec, points = pl.pallas_call(
        functools.partial(spectrum_kernel, n_row, n_src, chunks),
        out_shape=(
            jax.ShapeDtypeStruct((P_SIZE, 2 * P_SIZE), jnp.bfloat16),
            jax.ShapeDtypeStruct((n_src,) + own.shape, jnp.int32),
        ),
        in_specs=[anywhere, anywhere, anywhere, vmem],
        out_specs=(vmem, vmem),
        scratch_shapes=[
            pltpu.VMEM((rows, cols), jnp.bfloat16),
            pltpu.VMEM((cols, 2 * P_SIZE), jnp.bfloat16),
            pltpu.VMEM((2 * P_SIZE, rows), jnp.bfloat16),
            pltpu.VMEM((rows, 2 * P_SIZE), jnp.bfloat16),
            pltpu.VMEM((P_SIZE, 2 * P_SIZE), jnp.float32),
            pltpu.VMEM((P_SIZE, 2 * P_SIZE), jnp.bfloat16),
            pltpu.VMEM((n, per, 2 * P_SIZE), jnp.bfloat16),
            pltpu.SemaphoreType.DMA((chunks + 2,)),
            pltpu.SemaphoreType.DMA((n,)),
            pltpu.SemaphoreType.DMA((n,)),
            pltpu.SemaphoreType.DMA((n,)),
            pltpu.SemaphoreType.DMA((n,)),
            pltpu.SemaphoreType.DMA((n_src,)),
            pltpu.SemaphoreType.DMA((n_src,)),
        ],
        compiler_params=pltpu.CompilerParams(
            collective_id=0, has_side_effects=True, vmem_limit_bytes=40 * 2**20
        ),
        name="spectrum",
    )(
        mask_clip,
        jnp.asarray(forward_table(n_src * cols)),
        jnp.asarray(np.ascontiguousarray(forward_table(n_row * rows).T)),
        own,
    )
    row_table, col_table, high, low = inverse_tables(n)
    block = NI // n
    sources = n_src * own.shape[0]
    return pl.pallas_call(
        image_kernel,
        out_shape=jax.ShapeDtypeStruct((block, NI), jnp.float32),
        in_specs=[vmem, pl.BlockSpec(memory_space=pltpu.SMEM), anywhere, vmem, vmem, vmem],
        out_specs=vmem,
        scratch_shapes=[
            pltpu.VMEM((2 * P_SIZE, 2 * block), jnp.bfloat16),
            pltpu.VMEM((P_SIZE, 2 * P_SIZE), jnp.bfloat16),
            pltpu.VMEM((sources, 2 * P_SIZE, 2 * block), jnp.bfloat16),
            pltpu.VMEM((COARSE, block), jnp.float32),
            pltpu.SemaphoreType.DMA((1,)),
        ],
        compiler_params=pltpu.CompilerParams(vmem_limit_bytes=40 * 2**20),
        name="image",
    )(spec, points, jnp.asarray(row_table), jnp.asarray(col_table), jnp.asarray(high), jnp.asarray(low))


def solution(mesh):
    placed = (P(("clip", "row"), "src"), P("src", None), P("src"))
    return jax.shard_map(
        functools.partial(body, mesh.shape["row"], mesh.shape["src"]),
        mesh=mesh, in_specs=placed, out_specs=P(("clip", "row", "src"), None), check_vma=False,
    )
```

```python
import functools
import math

import jax
import jax.numpy as jnp
import ml_dtypes
import numpy as np
from jax import lax
from jax.experimental import pallas as pl
from jax.experimental.pallas import tpu as pltpu
from jax.sharding import PartitionSpec as P

P_SIZE = 256
NI = 1024
COARSE = 512
MESH = pl.DeviceIdType.MESH
BF16 = ml_dtypes.bfloat16


def twiddles(positions, length, scaling):
    frequency = np.arange(P_SIZE) - P_SIZE // 2
    angles = np.mod(positions[:, None] * frequency[None, :], length) * (2.0 * math.pi / length)
    return np.cos(angles) * scaling, np.sin(angles) * scaling


@functools.lru_cache(maxsize=None)
def forward_table(length):
    cos, sin = twiddles(np.arange(length), length, 1.0 / math.sqrt(length))
    return np.concatenate([cos, sin], 1).astype(np.float32).astype(BF16)


@functools.lru_cache(maxsize=None)
def row_table_of(length):
    table, h = forward_table(length).T, P_SIZE // 2
    rows = [table[:h], table[P_SIZE : P_SIZE + h], table[h : h + 1]]
    return np.concatenate(rows + [np.zeros((15, length), BF16)], 0)


@functools.lru_cache(maxsize=None)
def unfold_tables(n):
    p, h, width = P_SIZE, P_SIZE // 2, 2 * P_SIZE // n
    own, flip, side, zero = np.eye(p), np.zeros((p, p)), np.zeros((p, h)), np.zeros((p, h))
    flip[np.arange(1, p), p - np.arange(1, p)] = 1.0
    side[np.arange(p), h - width + np.arange(p) % width] = 1.0
    pick_re, pick_im = np.zeros((p, h)), np.zeros((p, h))
    pick_re[0, 0] = pick_im[0, 1] = 1.0
    real = np.block([[own, zero], [flip, pick_re], [np.zeros((p, p)), side]])
    imag = np.block([[own, zero], [-flip, pick_im], [np.zeros((p, p)), side]])
    back = np.zeros((p, h))
    back[h - np.arange(1, h), np.arange(1, h)] = 1.0
    back[h:, 0] = 1.0
    return np.stack([real, imag]).astype(BF16), back.astype(BF16)


@functools.lru_cache(maxsize=None)
def inverse_tables(row_blocks):
    cos, sin = twiddles(np.arange(NI), NI, 1.0 / math.sqrt(P_SIZE))
    cols = np.concatenate([cos, sin], 1)[:: NI // COARSE]
    block = NI // row_blocks
    rows = np.stack(
        [
            np.block([[c.T, s.T], [-s.T, c.T]])
            for c, s in zip(cos.reshape(-1, block, P_SIZE), sin.reshape(-1, block, P_SIZE))
        ]
    )
    band = P_SIZE // 2
    u = np.arange(-COARSE, COARSE + 1)
    ramp = np.clip((np.abs(u) - band) / (COARSE - 2 * band), 0.0, 1.0)
    gain = 0.5 + 0.5 * np.cos(math.pi * ramp)
    offset = np.arange(NI)
    kernel = (gain[None, :] * np.cos(2 * math.pi * offset[:, None] * u[None, :] / NI)).sum(1) / COARSE
    step = NI // COARSE
    spread = kernel[np.mod(np.arange(NI)[None, :] - step * np.arange(COARSE)[:, None], NI)]
    high = spread.astype(np.float32).astype(BF16)
    low = (spread - high.astype(np.float64)).astype(np.float32).astype(BF16)
    as_bf16 = lambda x: x.astype(np.float32).astype(BF16)
    return as_bf16(rows), as_bf16(cols), high, low


def spectrum_kernel(
    n_row, n_src, chunks,
    mask_hbm, col_hbm, row_hbm, own_shifts, own_weights,
    spec_ref, shifts_ref, weights_ref,
    mask, col, row, half, part, send, arrived,
    load_sem, rs_send, rs_recv, ag_send, ag_recv, pt_send, pt_recv,
):
    n = n_row * n_src
    row_id, src_id = lax.axis_index("row"), lax.axis_index("src")
    me = row_id * n_src + src_id
    rows, cols = mask.shape
    piece = rows // chunks
    per = P_SIZE // 2 // n

    loads = [
        pltpu.make_async_copy(
            col_hbm.at[pl.ds(pl.multiple_of(src_id * cols, cols), cols)], col, load_sem.at[0]
        )
    ]
    for i in range(chunks):
        loads.append(
            pltpu.make_async_copy(
                mask_hbm.at[pl.ds(i * piece, piece)], mask.at[pl.ds(i * piece, piece)],
                load_sem.at[1 + i],
            )
        )
    loads.append(
        pltpu.make_async_copy(
            row_hbm.at[:, pl.ds(pl.multiple_of(row_id * rows, rows), rows)], row,
            load_sem.at[1 + chunks],
        )
    )
    for load in loads:
        load.start()

    def partner(k):
        other = lax.rem(me + k, n)
        return other, {"row": other // n_src, "src": lax.rem(other, n_src)}

    barrier = pltpu.get_barrier_semaphore()
    for k in range(1, n):
        pl.semaphore_signal(barrier, inc=1, device_id=partner(k)[1], device_id_type=MESH)

    loads[0].wait()
    for i in range(chunks):
        loads[1 + i].wait()
        half[pl.ds(i * piece, piece)] = jnp.dot(
            mask[pl.ds(i * piece, piece)], col[...], preferred_element_type=jnp.float32
        ).astype(jnp.bfloat16)
    loads[-1].wait()
    blocks = jnp.dot(row[...], half[...], preferred_element_type=jnp.float32)
    p, h = P_SIZE, P_SIZE // 2
    cos_re, cos_im = blocks[:h, :p], -blocks[:h, p:]
    sin_re, sin_im = blocks[h:p, :p], -blocks[h:p, p:]
    part[:, :p] = cos_re + sin_im
    part[:, p : 2 * p] = cos_im - sin_re
    lane = lax.broadcasted_iota(jnp.int32, (h, h), 1)
    mirror_re, mirror_im = (cos_re - sin_im)[:, :1], (cos_im + sin_re)[:, :1]
    part[:, 2 * p :] = jnp.where(lane == 0, mirror_re, jnp.where(lane == 1, mirror_im, 0.0))
    middle = jnp.concatenate([blocks[p : p + 1, :p], -blocks[p : p + 1, p:]], 1)
    width = 2 * p // n
    for d in range(n):
        part[pl.ds(d * per, 1), 2 * p + h - width :] = middle[:, d * width : (d + 1) * width]
    send[...] = part[...].astype(jnp.bfloat16)

    pl.semaphore_wait(barrier, n - 1)
    outgoing = []
    for k in range(1, n):
        other, where = partner(k)
        copy = pltpu.make_async_remote_copy(
            src_ref=send.at[pl.ds(pl.multiple_of(other * per, per), per)],
            dst_ref=arrived.at[k],
            send_sem=rs_send.at[k], recv_sem=rs_recv.at[k],
            device_id=where, device_id_type=MESH,
        )
        copy.start()
        outgoing.append(copy)
    point_copies = []
    for k in range(1, n_src):
        for i, (own, everyone) in enumerate([(own_shifts, shifts_ref), (own_weights, weights_ref)]):
            copy = pltpu.make_async_remote_copy(
                src_ref=own, dst_ref=everyone.at[src_id],
                send_sem=pt_send.at[i, k], recv_sem=pt_recv.at[i, k],
                device_id={"src": lax.rem(src_id + k, n_src)}, device_id_type=MESH,
            )
            copy.start()
            point_copies.append(copy)
    shifts_ref[src_id] = own_shifts[...]
    weights_ref[src_id] = own_weights[...]

    mine = pl.ds(pl.multiple_of(me * per, per), per)
    total = part[mine]
    for k, copy in enumerate(outgoing, 1):
        copy.wait_recv()
        total = total + arrived[k].astype(jnp.float32)
    spec_ref[mine] = total.astype(jnp.bfloat16)
    gathered = []
    for k in range(1, n):
        copy = pltpu.make_async_remote_copy(
            src_ref=spec_ref.at[mine], dst_ref=spec_ref.at[mine],
            send_sem=ag_send.at[k], recv_sem=ag_recv.at[k],
            device_id=partner(k)[1], device_id_type=MESH,
        )
        copy.start()
        gathered.append(copy)
    for copy in point_copies + gathered:
        copy.wait_recv()
    for copy in outgoing + point_copies + gathered:
        copy.wait_send()


def image_kernel(
    spec_ref, shifts, weights, unfold_ref, back_ref, rows_hbm, col_ref, high_hbm, low_hbm,
    out_ref, rows, high_ref, low_ref, turned, halves, total, sem,
):
    n_src = lax.axis_size("src")
    me = lax.axis_index("row") * n_src + lax.axis_index("src")
    load = pltpu.make_async_copy(rows_hbm.at[me], rows, sem.at[0])
    load_high = pltpu.make_async_copy(high_hbm, high_ref, sem.at[1])
    load_low = pltpu.make_async_copy(low_hbm, low_ref, sem.at[2])
    load.start()
    load_high.start()
    load_low.start()
    p = P_SIZE
    block = out_ref.shape[0]
    per = weights.shape[2]
    sources = n_src * per
    h, width = p // 2, 2 * p // (NI // block)
    lane = lax.broadcasted_iota(jnp.int32, (p, h), 1)
    line = lax.broadcasted_iota(jnp.int32, (p, h), 0)
    chunk = h // (NI // block)
    for i in range(2):
        kept = jnp.concatenate([spec_ref[:, i * p : (i + 1) * p], spec_ref[:, 2 * p :]], 1)
        picked = lax.dot_general(
            unfold_ref[i], kept, (((1,), (1,)), ((), ())), preferred_element_type=jnp.float32
        )
        holder = (i * p + line) // width * chunk
        middle = jnp.where(lane == holder, picked[2 * p :], 0.0)
        mirrored = jnp.concatenate([picked[p : 2 * p], middle], 1).astype(jnp.bfloat16)
        upper = jnp.dot(mirrored, back_ref[...], preferred_element_type=jnp.float32)
        turned[:, i * p : i * p + h] = picked[:p].astype(jnp.bfloat16)
        turned[:, i * p + h : (i + 1) * p] = upper.astype(jnp.bfloat16)
    along_rows = lax.broadcasted_iota(jnp.int32, (p, p), 1) - p // 2
    along_cols = lax.broadcasted_iota(jnp.int32, (p, p), 0) - p // 2
    radius = p // 4
    load.wait()

    def first(s, carry):
        down = along_rows + shifts[s // per, 0, lax.rem(s, per)]
        across = along_cols + shifts[s // per, 1, lax.rem(s, per)]
        inside = down * down + across * across <= radius * radius
        pupil = jnp.where(inside, 1.0, 0.0).astype(jnp.bfloat16)
        passed = jnp.concatenate([turned[:, :p] * pupil, turned[:, p:] * pupil], 1)
        k = jnp.dot(passed, rows[...], preferred_element_type=jnp.float32).astype(jnp.bfloat16)
        halves[s, :p] = k
        halves[s, p:, :block] = -k[:, block:]
        halves[s, p:, block:] = k[:, :block]
        return carry

    lax.fori_loop(0, sources, first, 0, unroll=2)
    total[...] = jnp.zeros_like(total)

    def second(s, carry):
        weight = weights[s // per, 0, lax.rem(s, per)].astype(jnp.float32) * (1.0 / sources)
        e = jnp.dot(col_ref[...], halves[s], preferred_element_type=jnp.float32)
        total[...] += weight * (e[:, :block] * e[:, :block] + e[:, block:] * e[:, block:])
        return carry

    lax.fori_loop(0, sources, second, 0, unroll=2)
    load_high.wait()
    load_low.wait()
    summed = total[...].T
    top = summed.astype(jnp.bfloat16)
    rest = (summed - top.astype(jnp.float32)).astype(jnp.bfloat16)
    out_ref[...] = (
        jnp.dot(top, high_ref[...], preferred_element_type=jnp.float32)
        + jnp.dot(rest, high_ref[...], preferred_element_type=jnp.float32)
        + jnp.dot(top, low_ref[...], preferred_element_type=jnp.float32)
    )


def body(n_row, n_src, mask_clip, source_shifts, source_weights):
    n = n_row * n_src
    rows, cols = mask_clip.shape
    side = P_SIZE // 2
    kept = (side, 2 * P_SIZE + side)
    shifts, weights = source_shifts.T, source_weights[None, :]
    chunks = 4
    vmem = pl.BlockSpec(memory_space=pltpu.VMEM)
    smem = pl.BlockSpec(memory_space=pltpu.SMEM)
    hbm = pl.BlockSpec(memory_space=pltpu.HBM)
    spec, all_shifts, all_weights = pl.pallas_call(
        functools.partial(spectrum_kernel, n_row, n_src, chunks),
        out_shape=(
            jax.ShapeDtypeStruct(kept, jnp.bfloat16),
            jax.ShapeDtypeStruct((n_src,) + shifts.shape, jnp.int32),
            jax.ShapeDtypeStruct((n_src,) + weights.shape, jnp.int32),
        ),
        in_specs=[hbm, hbm, hbm, vmem, vmem],
        out_specs=(vmem, vmem, vmem),
        scratch_shapes=[
            pltpu.VMEM((rows, cols), jnp.bfloat16),
            pltpu.VMEM((cols, 2 * P_SIZE), jnp.bfloat16),
            pltpu.VMEM((P_SIZE + 16, rows), jnp.bfloat16),
            pltpu.VMEM((rows, 2 * P_SIZE), jnp.bfloat16),
            pltpu.VMEM(kept, jnp.float32),
            pltpu.VMEM(kept, jnp.bfloat16),
            pltpu.VMEM((n, side // n, kept[1]), jnp.bfloat16),
            pltpu.SemaphoreType.DMA((chunks + 2,)),
            pltpu.SemaphoreType.DMA((n,)),
            pltpu.SemaphoreType.DMA((n,)),
            pltpu.SemaphoreType.DMA((n,)),
            pltpu.SemaphoreType.DMA((n,)),
            pltpu.SemaphoreType.DMA((2, n_src)),
            pltpu.SemaphoreType.DMA((2, n_src)),
        ],
        compiler_params=pltpu.CompilerParams(
            collective_id=0, has_side_effects=True, vmem_limit_bytes=62 * 2**20
        ),
        name="spectrum",
    )(
        mask_clip,
        jnp.asarray(forward_table(n_src * cols)),
        jnp.asarray(row_table_of(n_row * rows)),
        shifts,
        weights,
    )
    row_table, col_table, high, low = inverse_tables(n)
    unfold, back = unfold_tables(n)
    block = NI // n
    sources = n_src * source_weights.shape[0]
    return pl.pallas_call(
        image_kernel,
        out_shape=jax.ShapeDtypeStruct((block, NI), jnp.float32),
        in_specs=[vmem, smem, smem, vmem, vmem, hbm, vmem, hbm, hbm],
        out_specs=vmem,
        scratch_shapes=[
            pltpu.VMEM((2 * P_SIZE, 2 * block), jnp.bfloat16),
            pltpu.VMEM((COARSE, NI), jnp.bfloat16),
            pltpu.VMEM((COARSE, NI), jnp.bfloat16),
            pltpu.VMEM((P_SIZE, 2 * P_SIZE), jnp.bfloat16),
            pltpu.VMEM((sources, 2 * P_SIZE, 2 * block), jnp.bfloat16),
            pltpu.VMEM((COARSE, block), jnp.float32),
            pltpu.SemaphoreType.DMA((3,)),
        ],
        compiler_params=pltpu.CompilerParams(vmem_limit_bytes=62 * 2**20),
        name="image",
    )(
        spec, all_shifts, all_weights,
        *map(jnp.asarray, (unfold, back, row_table, col_table, high, low)),
    )


def solution(mesh):
    placed = (P(("clip", "row"), "src"), P("src", None), P("src"))
    return jax.shard_map(
        functools.partial(body, mesh.shape["row"], mesh.shape["src"]),
        mesh=mesh, in_specs=placed, out_specs=P(("clip", "row", "src"), None), check_vma=False,
    )
```

```python
import functools
import math

import jax
import jax.numpy as jnp
import ml_dtypes
import numpy as np
from jax import lax
from jax.experimental import pallas as pl
from jax.experimental.pallas import tpu as pltpu
from jax.sharding import PartitionSpec as P

P_SIZE = 256
NI = 1024
COARSE = 384
MESH = pl.DeviceIdType.MESH
BF16 = ml_dtypes.bfloat16


def twiddles(positions, length, scaling):
    frequency = np.arange(P_SIZE) - P_SIZE // 2
    angles = np.mod(positions[:, None] * frequency[None, :], length) * (2.0 * math.pi / length)
    return np.cos(angles) * scaling, np.sin(angles) * scaling


@functools.lru_cache(maxsize=None)
def forward_table(length):
    cos, sin = twiddles(np.arange(length), length, 1.0 / math.sqrt(length))
    return np.concatenate([cos, sin], 1).astype(np.float32).astype(BF16)


@functools.lru_cache(maxsize=None)
def row_table_of(length):
    table, h = forward_table(length).T, P_SIZE // 2
    rows = [table[:h], table[P_SIZE : P_SIZE + h], table[h : h + 1]]
    return np.concatenate(rows + [np.zeros((P_SIZE - 1, length), BF16)], 0)


@functools.lru_cache(maxsize=None)
def unfold_tables(n):
    p, h, width = P_SIZE, P_SIZE // 2, 2 * P_SIZE // n
    own, flip, side, zero = np.eye(p), np.zeros((p, p)), np.zeros((p, h)), np.zeros((p, h))
    flip[np.arange(1, p), p - np.arange(1, p)] = 1.0
    side[np.arange(p), h - width + np.arange(p) % width] = 1.0
    pick_re, pick_im = np.zeros((p, h)), np.zeros((p, h))
    pick_re[0, 0] = pick_im[0, 1] = 1.0
    real = np.block([[own, zero], [flip, pick_re], [np.zeros((p, p)), side]])
    imag = np.block([[own, zero], [-flip, pick_im], [np.zeros((p, p)), side]])
    back = np.zeros((p, h))
    back[h - np.arange(1, h), np.arange(1, h)] = 1.0
    back[h:, 0] = 1.0
    return np.stack([real, imag]).astype(BF16), back.astype(BF16)


@functools.lru_cache(maxsize=None)
def inverse_tables(row_blocks):
    cos, sin = twiddles(np.arange(NI), NI, 1.0 / math.sqrt(P_SIZE))
    step = NI / COARSE
    cols = np.concatenate(twiddles(np.arange(COARSE) * step, NI, 1.0 / math.sqrt(P_SIZE)), 1)
    block = NI // row_blocks
    rows = np.stack(
        [
            np.block([[c.T, s.T], [-s.T, c.T]])
            for c, s in zip(cos.reshape(-1, block, P_SIZE), sin.reshape(-1, block, P_SIZE))
        ]
    )
    band = P_SIZE // 2
    u = np.arange(-COARSE, COARSE + 1)
    ramp = np.clip((np.abs(u) - band) / (COARSE - 2 * band), 0.0, 1.0)
    gain = 0.5 + 0.5 * np.cos(math.pi * ramp)
    offset = np.arange(NI)[None, :] - step * np.arange(COARSE)[:, None]
    spread = sum(g * np.cos(2 * math.pi / NI * v * offset) for g, v in zip(gain, u)) / COARSE
    high = spread.astype(np.float32).astype(BF16)
    low = (spread - high.astype(np.float64)).astype(np.float32).astype(BF16)
    as_bf16 = lambda x: x.astype(np.float32).astype(BF16)
    return as_bf16(rows), as_bf16(cols), high, low


def spectrum_kernel(
    n_row, n_src, chunks,
    mask_hbm, col_hbm, row_hbm, own_shifts, own_weights,
    spec_ref, shifts_ref, weights_ref,
    mask, col, row, half, part, send, arrived,
    load_sem, rs_send, rs_recv, ag_send, ag_recv, pt_send, pt_recv,
):
    n = n_row * n_src
    row_id, src_id = lax.axis_index("row"), lax.axis_index("src")
    me = row_id * n_src + src_id
    rows, cols = mask.shape
    piece = rows // chunks
    per = P_SIZE // 2 // n

    loads = [
        pltpu.make_async_copy(
            col_hbm.at[pl.ds(pl.multiple_of(src_id * cols, cols), cols)], col, load_sem.at[0]
        )
    ]
    for i in range(chunks):
        loads.append(
            pltpu.make_async_copy(
                mask_hbm.at[pl.ds(i * piece, piece)], mask.at[pl.ds(i * piece, piece)],
                load_sem.at[1 + i],
            )
        )
    loads.append(
        pltpu.make_async_copy(
            row_hbm.at[pl.ds(0, row.shape[0]), pl.ds(pl.multiple_of(row_id * rows, rows), rows)], row,
            load_sem.at[1 + chunks],
        )
    )
    for load in loads:
        load.start()

    def partner(k):
        other = lax.rem(me + k, n)
        return other, {"row": other // n_src, "src": lax.rem(other, n_src)}

    barrier = pltpu.get_barrier_semaphore()
    for k in range(1, n):
        pl.semaphore_signal(barrier, inc=1, device_id=partner(k)[1], device_id_type=MESH)

    loads[0].wait()
    for i in range(chunks):
        loads[1 + i].wait()
        half[pl.ds(i * piece, piece)] = jnp.dot(
            mask[pl.ds(i * piece, piece)], col[...], preferred_element_type=jnp.float32
        ).astype(jnp.bfloat16)
    loads[-1].wait()
    blocks = jnp.dot(row[...], half[...], preferred_element_type=jnp.float32)
    p, h = P_SIZE, P_SIZE // 2
    cos_re, cos_im = blocks[:h, :p], -blocks[:h, p:]
    sin_re, sin_im = blocks[h:p, :p], -blocks[h:p, p:]
    part[:, :p] = cos_re + sin_im
    part[:, p : 2 * p] = cos_im - sin_re
    lane = lax.broadcasted_iota(jnp.int32, (h, h), 1)
    mirror_re, mirror_im = (cos_re - sin_im)[:, :1], (cos_im + sin_re)[:, :1]
    part[:, 2 * p :] = jnp.where(lane == 0, mirror_re, jnp.where(lane == 1, mirror_im, 0.0))
    middle = jnp.concatenate([blocks[p : p + 1, :p], -blocks[p : p + 1, p:]], 1)
    width = 2 * p // n
    for d in range(n):
        part[pl.ds(d * per, 1), 2 * p + h - width :] = middle[:, d * width : (d + 1) * width]
    send[...] = part[...].astype(jnp.bfloat16)

    pl.semaphore_wait(barrier, n - 1)
    outgoing = []
    for k in range(1, n):
        other, where = partner(k)
        copy = pltpu.make_async_remote_copy(
            src_ref=send.at[pl.ds(pl.multiple_of(other * per, per), per)],
            dst_ref=arrived.at[k],
            send_sem=rs_send.at[k], recv_sem=rs_recv.at[k],
            device_id=where, device_id_type=MESH,
        )
        copy.start()
        outgoing.append(copy)
    point_copies = []
    for k in range(1, n_src):
        for i, (own, everyone) in enumerate([(own_shifts, shifts_ref), (own_weights, weights_ref)]):
            copy = pltpu.make_async_remote_copy(
                src_ref=own, dst_ref=everyone.at[src_id],
                send_sem=pt_send.at[i, k], recv_sem=pt_recv.at[i, k],
                device_id={"src": lax.rem(src_id + k, n_src)}, device_id_type=MESH,
            )
            copy.start()
            point_copies.append(copy)
    shifts_ref[src_id] = own_shifts[...]
    weights_ref[src_id] = own_weights[...]

    mine = pl.ds(pl.multiple_of(me * per, per), per)
    total = part[mine]
    for k, copy in enumerate(outgoing, 1):
        copy.wait_recv()
        total = total + arrived[k].astype(jnp.float32)
    spec_ref[mine] = total.astype(jnp.bfloat16)
    gathered = []
    for k in range(1, n):
        copy = pltpu.make_async_remote_copy(
            src_ref=spec_ref.at[mine], dst_ref=spec_ref.at[mine],
            send_sem=ag_send.at[k], recv_sem=ag_recv.at[k],
            device_id=partner(k)[1], device_id_type=MESH,
        )
        copy.start()
        gathered.append(copy)
    for copy in point_copies + gathered:
        copy.wait_recv()
    for copy in outgoing + point_copies + gathered:
        copy.wait_send()


def image_kernel(
    spec_ref, shifts, weights, unfold_ref, back_ref, rows_hbm, col_ref, high_hbm, low_hbm,
    out_ref, rows, high_ref, low_ref, turned, halves, total, sem,
):
    n_src = lax.axis_size("src")
    me = lax.axis_index("row") * n_src + lax.axis_index("src")
    load = pltpu.make_async_copy(rows_hbm.at[me], rows, sem.at[0])
    load_high = pltpu.make_async_copy(high_hbm, high_ref, sem.at[1])
    load_low = pltpu.make_async_copy(low_hbm, low_ref, sem.at[2])
    load.start()
    load_high.start()
    load_low.start()
    p = P_SIZE
    block = out_ref.shape[0]
    per = weights.shape[2]
    sources = n_src * per
    h, width = p // 2, 2 * p // (NI // block)
    lane = lax.broadcasted_iota(jnp.int32, (p, h), 1)
    line = lax.broadcasted_iota(jnp.int32, (p, h), 0)
    chunk = h // (NI // block)
    for i in range(2):
        kept = jnp.concatenate([spec_ref[:, i * p : (i + 1) * p], spec_ref[:, 2 * p :]], 1)
        picked = lax.dot_general(
            unfold_ref[i], kept, (((1,), (1,)), ((), ())), preferred_element_type=jnp.float32
        )
        holder = (i * p + line) // width * chunk
        middle = jnp.where(lane == holder, picked[2 * p :], 0.0)
        mirrored = jnp.concatenate([picked[p : 2 * p], middle], 1).astype(jnp.bfloat16)
        upper = jnp.dot(mirrored, back_ref[...], preferred_element_type=jnp.float32)
        turned[:, i * p : i * p + h] = picked[:p].astype(jnp.bfloat16)
        turned[:, i * p + h : (i + 1) * p] = upper.astype(jnp.bfloat16)
    along_rows = lax.broadcasted_iota(jnp.int32, (p, p), 1) - p // 2
    along_cols = lax.broadcasted_iota(jnp.int32, (p, p), 0) - p // 2
    radius = p // 4
    load.wait()

    def first(s, carry):
        down = along_rows + shifts[s // per, 0, lax.rem(s, per)]
        across = along_cols + shifts[s // per, 1, lax.rem(s, per)]
        inside = down * down + across * across <= radius * radius
        pupil = jnp.where(inside, 1.0, 0.0).astype(jnp.bfloat16)
        passed = jnp.concatenate([turned[:, :p] * pupil, turned[:, p:] * pupil], 1)
        k = jnp.dot(passed, rows[...], preferred_element_type=jnp.float32).astype(jnp.bfloat16)
        halves[s, :p] = k
        halves[s, p:, :block] = -k[:, block:]
        halves[s, p:, block:] = k[:, :block]
        return carry

    lax.fori_loop(0, sources, first, 0, unroll=16)
    total[...] = jnp.zeros_like(total)

    def second(s, carry):
        weight = weights[s // per, 0, lax.rem(s, per)].astype(jnp.float32) * (1.0 / sources)
        e = jnp.dot(col_ref[...], halves[s], preferred_element_type=jnp.float32)
        total[...] += weight * (e[:, :block] * e[:, :block] + e[:, block:] * e[:, block:])
        return carry

    lax.fori_loop(0, sources, second, 0, unroll=16)
    load_high.wait()
    load_low.wait()
    summed = total[...].T
    top = summed.astype(jnp.bfloat16)
    rest = (summed - top.astype(jnp.float32)).astype(jnp.bfloat16)
    out_ref[...] = (
        jnp.dot(top, high_ref[...], preferred_element_type=jnp.float32)
        + jnp.dot(rest, high_ref[...], preferred_element_type=jnp.float32)
        + jnp.dot(top, low_ref[...], preferred_element_type=jnp.float32)
    )


def body(n_row, n_src, mask_clip, source_shifts, source_weights):
    n = n_row * n_src
    rows, cols = mask_clip.shape
    side = P_SIZE // 2
    kept = (side, 2 * P_SIZE + side)
    shifts, weights = source_shifts.T, source_weights[None, :]
    chunks = 4
    vmem = pl.BlockSpec(memory_space=pltpu.VMEM)
    smem = pl.BlockSpec(memory_space=pltpu.SMEM)
    hbm = pl.BlockSpec(memory_space=pltpu.HBM)
    spec, all_shifts, all_weights = pl.pallas_call(
        functools.partial(spectrum_kernel, n_row, n_src, chunks),
        out_shape=(
            jax.ShapeDtypeStruct(kept, jnp.bfloat16),
            jax.ShapeDtypeStruct((n_src,) + shifts.shape, jnp.int32),
            jax.ShapeDtypeStruct((n_src,) + weights.shape, jnp.int32),
        ),
        in_specs=[hbm, hbm, hbm, vmem, vmem],
        out_specs=(vmem, vmem, vmem),
        scratch_shapes=[
            pltpu.VMEM((rows, cols), jnp.bfloat16),
            pltpu.VMEM((cols, 2 * P_SIZE), jnp.bfloat16),
            pltpu.VMEM((P_SIZE + 16, rows), jnp.bfloat16),
            pltpu.VMEM((rows, 2 * P_SIZE), jnp.bfloat16),
            pltpu.VMEM(kept, jnp.float32),
            pltpu.VMEM(kept, jnp.bfloat16),
            pltpu.VMEM((n, side // n, kept[1]), jnp.bfloat16),
            pltpu.SemaphoreType.DMA((chunks + 2,)),
            pltpu.SemaphoreType.DMA((n,)),
            pltpu.SemaphoreType.DMA((n,)),
            pltpu.SemaphoreType.DMA((n,)),
            pltpu.SemaphoreType.DMA((n,)),
            pltpu.SemaphoreType.DMA((2, n_src)),
            pltpu.SemaphoreType.DMA((2, n_src)),
        ],
        compiler_params=pltpu.CompilerParams(
            collective_id=0, has_side_effects=True, vmem_limit_bytes=62 * 2**20
        ),
        name="spectrum",
    )(
        mask_clip,
        jnp.asarray(forward_table(n_src * cols)),
        jnp.asarray(row_table_of(n_row * rows)),
        shifts,
        weights,
    )
    row_table, col_table, high, low = inverse_tables(n)
    unfold, back = unfold_tables(n)
    block = NI // n
    sources = n_src * source_weights.shape[0]
    return pl.pallas_call(
        image_kernel,
        out_shape=jax.ShapeDtypeStruct((block, NI), jnp.float32),
        in_specs=[vmem, smem, smem, vmem, vmem, hbm, vmem, hbm, hbm],
        out_specs=vmem,
        scratch_shapes=[
            pltpu.VMEM((2 * P_SIZE, 2 * block), jnp.bfloat16),
            pltpu.VMEM((COARSE, NI), jnp.bfloat16),
            pltpu.VMEM((COARSE, NI), jnp.bfloat16),
            pltpu.VMEM((P_SIZE, 2 * P_SIZE), jnp.bfloat16),
            pltpu.VMEM((sources, 2 * P_SIZE, 2 * block), jnp.bfloat16),
            pltpu.VMEM((COARSE, block), jnp.float32),
            pltpu.SemaphoreType.DMA((3,)),
        ],
        compiler_params=pltpu.CompilerParams(vmem_limit_bytes=62 * 2**20),
        name="image",
    )(
        spec, all_shifts, all_weights,
        *map(jnp.asarray, (unfold, back, row_table, col_table, high, low)),
    )


def solution(mesh):
    placed = (P(("clip", "row"), "src"), P("src", None), P("src"))
    return jax.shard_map(
        functools.partial(body, mesh.shape["row"], mesh.shape["src"]),
        mesh=mesh, in_specs=placed, out_specs=P(("clip", "row", "src"), None), check_vma=False,
    )
```

```python
import functools
import math

import jax
import jax.numpy as jnp
import ml_dtypes
import numpy as np
from jax import lax
from jax.experimental import pallas as pl
from jax.experimental.pallas import tpu as pltpu
from jax.sharding import PartitionSpec as P

P_SIZE = 256
NI = 1024
COARSE = 384
MESH = pl.DeviceIdType.MESH
BF16 = ml_dtypes.bfloat16


def twiddles(positions, length, scaling):
    frequency = np.arange(P_SIZE) - P_SIZE // 2
    angles = np.mod(positions[:, None] * frequency[None, :], length) * (2.0 * math.pi / length)
    return np.cos(angles) * scaling, np.sin(angles) * scaling


@functools.lru_cache(maxsize=None)
def forward_table(length):
    cos, sin = twiddles(np.arange(length), length, 1.0 / math.sqrt(length))
    return np.concatenate([cos, sin], 1).astype(np.float32).astype(BF16)


@functools.lru_cache(maxsize=None)
def row_table_of(length):
    table, h = forward_table(length).T, P_SIZE // 2
    rows = [table[:h], table[P_SIZE : P_SIZE + h], table[h : h + 1]]
    return np.concatenate(rows + [np.zeros((P_SIZE - 1, length), BF16)], 0)


@functools.lru_cache(maxsize=None)
def unfold_tables(n):
    p, h, width = P_SIZE, P_SIZE // 2, 2 * P_SIZE // n
    own, flip, side, zero = np.eye(p), np.zeros((p, p)), np.zeros((p, h)), np.zeros((p, h))
    flip[np.arange(1, p), p - np.arange(1, p)] = 1.0
    side[np.arange(p), h - width + np.arange(p) % width] = 1.0
    pick_re, pick_im = np.zeros((p, h)), np.zeros((p, h))
    pick_re[0, 0] = pick_im[0, 1] = 1.0
    real = np.block([[own, zero], [flip, pick_re], [np.zeros((p, p)), side]])
    imag = np.block([[own, zero], [-flip, pick_im], [np.zeros((p, p)), side]])
    back = np.zeros((p, h))
    back[h - np.arange(1, h), np.arange(1, h)] = 1.0
    back[h:, 0] = 1.0
    return np.stack([real, imag]).astype(BF16), back.astype(BF16)


@functools.lru_cache(maxsize=None)
def inverse_tables(row_blocks):
    cos, sin = twiddles(np.arange(NI), NI, 1.0 / math.sqrt(P_SIZE))
    step = NI / COARSE
    cols = np.concatenate(twiddles(np.arange(COARSE) * step, NI, 1.0 / math.sqrt(P_SIZE)), 1)
    block = NI // row_blocks
    rows = np.stack(
        [
            np.block([[c.T, s.T], [-s.T, c.T]])
            for c, s in zip(cos.reshape(-1, block, P_SIZE), sin.reshape(-1, block, P_SIZE))
        ]
    )
    band = P_SIZE // 2
    u = np.arange(-COARSE, COARSE + 1)
    ramp = np.clip((np.abs(u) - band) / (COARSE - 2 * band), 0.0, 1.0)
    gain = 0.5 + 0.5 * np.cos(math.pi * ramp)
    offset = np.arange(NI)[None, :] - step * np.arange(COARSE)[:, None]
    spread = sum(g * np.cos(2 * math.pi / NI * v * offset) for g, v in zip(gain, u)) / COARSE
    high = spread.astype(np.float32).astype(BF16)
    low = (spread - high.astype(np.float64)).astype(np.float32).astype(BF16)
    as_bf16 = lambda x: x.astype(np.float32).astype(BF16)
    return as_bf16(rows), as_bf16(cols), high, low


def kernel(
    n_row, n_src, chunks,
    mask_hbm, col_hbm, row_hbm, own_shifts, own_weights,
    unfold_hbm, back_hbm, rows_hbm, col_ref_hbm, total,
    mask, col, row, half, part, send, arrived,
    spec_ref, shifts_ref, weights_ref, shifts, weights,
    unfold_ref, back_ref, image_rows, col_ref, pupils, turned, halves,
    load_sem, table_sem, point_sem, rs_send, rs_recv, ag_send, ag_recv, pt_send, pt_recv,
):
    n = n_row * n_src
    row_id, src_id = lax.axis_index("row"), lax.axis_index("src")
    me = row_id * n_src + src_id
    rows, cols = mask.shape
    piece = rows // chunks
    per = P_SIZE // 2 // n

    loads = [
        pltpu.make_async_copy(
            col_hbm.at[pl.ds(pl.multiple_of(src_id * cols, cols), cols)], col, load_sem.at[0]
        )
    ]
    for i in range(chunks):
        loads.append(
            pltpu.make_async_copy(
                mask_hbm.at[pl.ds(i * piece, piece)], mask.at[pl.ds(i * piece, piece)],
                load_sem.at[1 + i],
            )
        )
    loads.append(
        pltpu.make_async_copy(
            row_hbm.at[pl.ds(0, row.shape[0]), pl.ds(pl.multiple_of(row_id * rows, rows), rows)], row,
            load_sem.at[1 + chunks],
        )
    )
    for load in loads:
        load.start()
    tables = [
        pltpu.make_async_copy(there, here, table_sem.at[i])
        for i, (there, here) in enumerate(
            [
                (unfold_hbm, unfold_ref), (back_hbm, back_ref), (rows_hbm.at[me], image_rows),
                (col_ref_hbm, col_ref),
            ]
        )
    ]

    def partner(k):
        other = lax.rem(me + k, n)
        return other, {"row": other // n_src, "src": lax.rem(other, n_src)}

    barrier = pltpu.get_barrier_semaphore()
    for k in range(1, n):
        pl.semaphore_signal(barrier, inc=1, device_id=partner(k)[1], device_id_type=MESH)

    loads[0].wait()
    for i in range(chunks):
        loads[1 + i].wait()
        half[pl.ds(i * piece, piece)] = jnp.dot(
            mask[pl.ds(i * piece, piece)], col[...], preferred_element_type=jnp.float32
        ).astype(jnp.bfloat16)
    loads[-1].wait()
    for table in tables:
        table.start()
    blocks = jnp.dot(row[...], half[...], preferred_element_type=jnp.float32)
    p, h = P_SIZE, P_SIZE // 2
    cos_re, cos_im = blocks[:h, :p], -blocks[:h, p:]
    sin_re, sin_im = blocks[h:p, :p], -blocks[h:p, p:]
    part[:, :p] = cos_re + sin_im
    part[:, p : 2 * p] = cos_im - sin_re
    lane = lax.broadcasted_iota(jnp.int32, (h, h), 1)
    mirror_re, mirror_im = (cos_re - sin_im)[:, :1], (cos_im + sin_re)[:, :1]
    part[:, 2 * p :] = jnp.where(lane == 0, mirror_re, jnp.where(lane == 1, mirror_im, 0.0))
    middle = jnp.concatenate([blocks[p : p + 1, :p], -blocks[p : p + 1, p:]], 1)
    width = 2 * p // n
    for d in range(n):
        part[pl.ds(d * per, 1), 2 * p + h - width :] = middle[:, d * width : (d + 1) * width]
    send[...] = part[...].astype(jnp.bfloat16)

    pl.semaphore_wait(barrier, n - 1)
    point_copies = []
    for k in range(1, n_src):
        for i, (own, everyone) in enumerate([(own_shifts, shifts_ref), (own_weights, weights_ref)]):
            copy = pltpu.make_async_remote_copy(
                src_ref=own, dst_ref=everyone.at[src_id],
                send_sem=pt_send.at[i, k], recv_sem=pt_recv.at[i, k],
                device_id={"src": lax.rem(src_id + k, n_src)}, device_id_type=MESH,
            )
            copy.start()
            point_copies.append(copy)
    shifts_ref[src_id] = own_shifts[...]
    weights_ref[src_id] = own_weights[...]
    outgoing = []
    for k in range(1, n):
        other, where = partner(k)
        copy = pltpu.make_async_remote_copy(
            src_ref=send.at[pl.ds(pl.multiple_of(other * per, per), per)],
            dst_ref=arrived.at[k],
            send_sem=rs_send.at[k], recv_sem=rs_recv.at[k],
            device_id=where, device_id_type=MESH,
        )
        copy.start()
        outgoing.append(copy)
    for copy in point_copies:
        copy.wait_recv()
    to_scalars = [
        pltpu.make_async_copy(shifts_ref, shifts, point_sem.at[0]),
        pltpu.make_async_copy(weights_ref, weights, point_sem.at[1]),
    ]
    for copy in to_scalars:
        copy.start()
    for copy in to_scalars:
        copy.wait()
    sources, count = pupils.shape[0], weights.shape[2]
    along_rows = lax.broadcasted_iota(jnp.int32, (p, p), 1) - h
    along_cols = lax.broadcasted_iota(jnp.int32, (p, p), 0) - h
    radius = p // 4

    def make_pupil(s, carry):
        down = along_rows + shifts[s // count, 0, lax.rem(s, count)]
        across = along_cols + shifts[s // count, 1, lax.rem(s, count)]
        inside = down * down + across * across <= radius * radius
        pupils[s] = jnp.where(inside, 1.0, 0.0).astype(jnp.bfloat16)
        return carry

    lax.fori_loop(0, sources, make_pupil, 0)

    mine = pl.ds(pl.multiple_of(me * per, per), per)
    reduced = part[mine]
    for k, copy in enumerate(outgoing, 1):
        copy.wait_recv()
        reduced = reduced + arrived[k].astype(jnp.float32)
    spec_ref[mine] = reduced.astype(jnp.bfloat16)
    gathered = []
    for k in range(1, n):
        copy = pltpu.make_async_remote_copy(
            src_ref=spec_ref.at[mine], dst_ref=spec_ref.at[mine],
            send_sem=ag_send.at[k], recv_sem=ag_recv.at[k],
            device_id=partner(k)[1], device_id_type=MESH,
        )
        copy.start()
        gathered.append(copy)
    for copy in gathered:
        copy.wait_recv()
    for copy in outgoing + point_copies + gathered:
        copy.wait_send()

    for table in tables:
        table.wait()
    block = total.shape[1]
    lane = lax.broadcasted_iota(jnp.int32, (p, h), 1)
    line = lax.broadcasted_iota(jnp.int32, (p, h), 0)
    for i in range(2):
        kept = jnp.concatenate([spec_ref[:, i * p : (i + 1) * p], spec_ref[:, 2 * p :]], 1)
        picked = lax.dot_general(
            unfold_ref[i], kept, (((1,), (1,)), ((), ())), preferred_element_type=jnp.float32
        )
        holder = (i * p + line) // width * per
        middle = jnp.where(lane == holder, picked[2 * p :], 0.0)
        mirrored = jnp.concatenate([picked[p : 2 * p], middle], 1).astype(jnp.bfloat16)
        upper = jnp.dot(mirrored, back_ref[...], preferred_element_type=jnp.float32)
        turned[:, i * p : i * p + h] = picked[:p].astype(jnp.bfloat16)
        turned[:, i * p + h : (i + 1) * p] = upper.astype(jnp.bfloat16)

    def first(s, carry):
        pupil = pupils[s]
        passed = jnp.concatenate([turned[:, :p] * pupil, turned[:, p:] * pupil], 1)
        k = jnp.dot(passed, image_rows[...], preferred_element_type=jnp.float32).astype(jnp.bfloat16)
        halves[s, :p] = k
        halves[s, p:, :block] = -k[:, block:]
        halves[s, p:, block:] = k[:, :block]
        return carry

    lax.fori_loop(0, sources, first, 0, unroll=16)
    total[...] = jnp.zeros_like(total)

    def second(s, carry):
        weight = weights[s // count, 0, lax.rem(s, count)].astype(jnp.float32) * (1.0 / sources)
        e = jnp.dot(col_ref[...], halves[s], preferred_element_type=jnp.float32)
        total[...] += weight * (e[:, :block] * e[:, :block] + e[:, block:] * e[:, block:])
        return carry

    lax.fori_loop(0, sources, second, 0, unroll=16)


def spread_kernel(total, high_ref, low_ref, out_ref):
    summed = total[...].T
    top = summed.astype(jnp.bfloat16)
    rest = (summed - top.astype(jnp.float32)).astype(jnp.bfloat16)
    out_ref[...] = (
        jnp.dot(top, high_ref[...], preferred_element_type=jnp.float32)
        + jnp.dot(rest, high_ref[...], preferred_element_type=jnp.float32)
        + jnp.dot(top, low_ref[...], preferred_element_type=jnp.float32)
    )


def body(n_row, n_src, mask_clip, source_shifts, source_weights):
    n = n_row * n_src
    rows, cols = mask_clip.shape
    side = P_SIZE // 2
    kept = (side, 2 * P_SIZE + side)
    shifts, weights = source_shifts.T, source_weights[None, :]
    chunks = 4
    vmem = pl.BlockSpec(memory_space=pltpu.VMEM)
    hbm = pl.BlockSpec(memory_space=pltpu.HBM)
    unfold, back = unfold_tables(n)
    row_table, col_table, high, low = inverse_tables(n)
    block = NI // n
    count = source_weights.shape[0]
    sources = n_src * count
    total = pl.pallas_call(
        functools.partial(kernel, n_row, n_src, chunks),
        out_shape=jax.ShapeDtypeStruct((COARSE, block), jnp.float32),
        in_specs=[hbm] * 3 + [vmem] * 2 + [hbm] * 4,
        out_specs=vmem,
        scratch_shapes=[
            pltpu.VMEM((rows, cols), jnp.bfloat16),
            pltpu.VMEM((cols, 2 * P_SIZE), jnp.bfloat16),
            pltpu.VMEM((P_SIZE + 16, rows), jnp.bfloat16),
            pltpu.VMEM((rows, 2 * P_SIZE), jnp.bfloat16),
            pltpu.VMEM(kept, jnp.float32),
            pltpu.VMEM(kept, jnp.bfloat16),
            pltpu.VMEM((n, side // n, kept[1]), jnp.bfloat16),
            pltpu.VMEM(kept, jnp.bfloat16),
            pltpu.VMEM((n_src, 2, count), jnp.int32),
            pltpu.VMEM((n_src, 1, count), jnp.int32),
            pltpu.SMEM((n_src, 2, count), jnp.int32),
            pltpu.SMEM((n_src, 1, count), jnp.int32),
            pltpu.VMEM(unfold.shape, jnp.bfloat16),
            pltpu.VMEM(back.shape, jnp.bfloat16),
            pltpu.VMEM((2 * P_SIZE, 2 * block), jnp.bfloat16),
            pltpu.VMEM(col_table.shape, jnp.bfloat16),
            pltpu.VMEM((sources, P_SIZE, P_SIZE), jnp.bfloat16),
            pltpu.VMEM((P_SIZE, 2 * P_SIZE), jnp.bfloat16),
            pltpu.VMEM((sources, 2 * P_SIZE, 2 * block), jnp.bfloat16),
            pltpu.SemaphoreType.DMA((chunks + 2,)),
            pltpu.SemaphoreType.DMA((4,)),
            pltpu.SemaphoreType.DMA((2,)),
            pltpu.SemaphoreType.DMA((n,)),
            pltpu.SemaphoreType.DMA((n,)),
            pltpu.SemaphoreType.DMA((n,)),
            pltpu.SemaphoreType.DMA((n,)),
            pltpu.SemaphoreType.DMA((2, n_src)),
            pltpu.SemaphoreType.DMA((2, n_src)),
        ],
        compiler_params=pltpu.CompilerParams(
            collective_id=0, has_side_effects=True, vmem_limit_bytes=62 * 2**20
        ),
        name="image",
    )(
        mask_clip,
        jnp.asarray(forward_table(n_src * cols)),
        jnp.asarray(row_table_of(n_row * rows)),
        shifts,
        weights,
        *map(jnp.asarray, (unfold, back, row_table, col_table)),
    )
    return pl.pallas_call(
        spread_kernel,
        out_shape=jax.ShapeDtypeStruct((block, NI), jnp.float32),
        in_specs=[vmem] * 3,
        out_specs=vmem,
        compiler_params=pltpu.CompilerParams(vmem_limit_bytes=62 * 2**20),
        name="spread",
    )(total, jnp.asarray(high), jnp.asarray(low))


def solution(mesh):
    placed = (P(("clip", "row"), "src"), P("src", None), P("src"))
    return jax.shard_map(
        functools.partial(body, mesh.shape["row"], mesh.shape["src"]),
        mesh=mesh, in_specs=placed, out_specs=P(("clip", "row", "src"), None), check_vma=False,
    )
```

```python
import functools
import math

import jax
import jax.numpy as jnp
import ml_dtypes
import numpy as np
from jax import lax
from jax.experimental import pallas as pl
from jax.experimental.pallas import tpu as pltpu
from jax.sharding import PartitionSpec as P

P_SIZE = 256
NI = 1024
COARSE = 384
MESH = pl.DeviceIdType.MESH
BF16 = ml_dtypes.bfloat16


def twiddles(positions, length, scaling):
    frequency = np.arange(P_SIZE) - P_SIZE // 2
    angles = np.mod(positions[:, None] * frequency[None, :], length) * (2.0 * math.pi / length)
    return np.cos(angles) * scaling, np.sin(angles) * scaling


@functools.lru_cache(maxsize=None)
def forward_table(length):
    cos, sin = twiddles(np.arange(length), length, 1.0 / math.sqrt(length))
    return np.concatenate([cos, sin], 1).astype(np.float32).astype(BF16)


@functools.lru_cache(maxsize=None)
def row_table_of(length):
    table, h = forward_table(length).T, P_SIZE // 2
    rows = [table[:h], table[P_SIZE : P_SIZE + h], table[h : h + 1]]
    return np.concatenate(rows + [np.zeros((P_SIZE - 1, length), BF16)], 0)


@functools.lru_cache(maxsize=None)
def unfold_tables(n):
    p, h, width = P_SIZE, P_SIZE // 2, 2 * P_SIZE // n
    own, flip, side, zero = np.eye(p), np.zeros((p, p)), np.zeros((p, h)), np.zeros((p, h))
    flip[np.arange(1, p), p - np.arange(1, p)] = 1.0
    side[np.arange(p), h - width + np.arange(p) % width] = 1.0
    pick_re, pick_im = np.zeros((p, h)), np.zeros((p, h))
    pick_re[0, 0] = pick_im[0, 1] = 1.0
    real = np.block([[own, zero], [flip, pick_re], [np.zeros((p, p)), side]])
    imag = np.block([[own, zero], [-flip, pick_im], [np.zeros((p, p)), side]])
    back = np.zeros((p, h))
    back[h - np.arange(1, h), np.arange(1, h)] = 1.0
    back[h:, 0] = 1.0
    return np.stack([real, imag]).astype(BF16), back.astype(BF16)


@functools.lru_cache(maxsize=None)
def inverse_tables(row_blocks):
    cos, sin = twiddles(np.arange(NI), NI, 1.0 / math.sqrt(P_SIZE))
    step = NI / COARSE
    cols = np.concatenate(twiddles(np.arange(COARSE) * step, NI, 1.0 / math.sqrt(P_SIZE)), 1)
    block = NI // row_blocks
    rows = np.stack(
        [
            np.block([[c.T, s.T], [-s.T, c.T]])
            for c, s in zip(cos.reshape(-1, block, P_SIZE), sin.reshape(-1, block, P_SIZE))
        ]
    )
    band = P_SIZE // 2
    u = np.arange(-COARSE, COARSE + 1)
    ramp = np.clip((np.abs(u) - band) / (COARSE - 2 * band), 0.0, 1.0)
    gain = 0.5 + 0.5 * np.cos(math.pi * ramp)
    offset = np.arange(NI)[None, :] - step * np.arange(COARSE)[:, None]
    spread = sum(g * np.cos(2 * math.pi / NI * v * offset) for g, v in zip(gain, u)) / COARSE
    high = spread.astype(np.float32).astype(BF16)
    low = (spread - high.astype(np.float64)).astype(np.float32).astype(BF16)
    as_bf16 = lambda x: x.astype(np.float32).astype(BF16)
    return as_bf16(rows), as_bf16(cols), high, low


def kernel(
    n_row, n_src, chunks,
    mask_hbm, col_hbm, row_hbm, own_shifts, own_weights,
    unfold_hbm, back_hbm, rows_hbm, col_ref_hbm, total,
    mask, col, row, half, part, send, arrived,
    spec_ref, shifts_ref, weights_ref, shifts, weights,
    unfold_ref, back_ref, image_rows, col_ref, pupils, turned, halves,
    load_sem, table_sem, point_sem, rs_send, rs_recv, ag_send, ag_recv, pt_send, pt_recv,
):
    n = n_row * n_src
    row_id, src_id = lax.axis_index("row"), lax.axis_index("src")
    me = row_id * n_src + src_id
    rows, cols = mask.shape
    piece = rows // chunks
    per = P_SIZE // 2 // n

    loads = [
        pltpu.make_async_copy(
            col_hbm.at[pl.ds(pl.multiple_of(src_id * cols, cols), cols)], col, load_sem.at[0]
        )
    ]
    for i in range(chunks):
        loads.append(
            pltpu.make_async_copy(
                mask_hbm.at[pl.ds(i * piece, piece)], mask.at[pl.ds(i * piece, piece)],
                load_sem.at[1 + i],
            )
        )
    loads.append(
        pltpu.make_async_copy(
            row_hbm.at[pl.ds(0, row.shape[0]), pl.ds(pl.multiple_of(row_id * rows, rows), rows)], row,
            load_sem.at[1 + chunks],
        )
    )
    for load in loads:
        load.start()
    tables = [
        pltpu.make_async_copy(there, here, table_sem.at[i])
        for i, (there, here) in enumerate(
            [
                (unfold_hbm, unfold_ref), (back_hbm, back_ref), (rows_hbm.at[me], image_rows),
                (col_ref_hbm, col_ref),
            ]
        )
    ]

    def partner(k):
        other = lax.rem(me + k, n)
        return other, {"row": other // n_src, "src": lax.rem(other, n_src)}

    barrier = pltpu.get_barrier_semaphore()
    for k in range(1, n):
        pl.semaphore_signal(barrier, inc=1, device_id=partner(k)[1], device_id_type=MESH)

    loads[0].wait()
    for i in range(chunks):
        loads[1 + i].wait()
        half[pl.ds(i * piece, piece)] = jnp.dot(
            mask[pl.ds(i * piece, piece)], col[...], preferred_element_type=jnp.float32
        ).astype(jnp.bfloat16)
    loads[-1].wait()
    for table in tables:
        table.start()
    blocks = jnp.dot(row[...], half[...], preferred_element_type=jnp.float32)
    p, h = P_SIZE, P_SIZE // 2
    cos_re, cos_im = blocks[:h, :p], -blocks[:h, p:]
    sin_re, sin_im = blocks[h:p, :p], -blocks[h:p, p:]
    part[:, :p] = cos_re + sin_im
    part[:, p : 2 * p] = cos_im - sin_re
    lane = lax.broadcasted_iota(jnp.int32, (h, h), 1)
    mirror_re, mirror_im = (cos_re - sin_im)[:, :1], (cos_im + sin_re)[:, :1]
    part[:, 2 * p :] = jnp.where(lane == 0, mirror_re, jnp.where(lane == 1, mirror_im, 0.0))
    middle = jnp.concatenate([blocks[p : p + 1, :p], -blocks[p : p + 1, p:]], 1)
    width = 2 * p // n
    for d in range(n):
        part[pl.ds(d * per, 1), 2 * p + h - width :] = middle[:, d * width : (d + 1) * width]
    send[...] = part[...].astype(jnp.bfloat16)

    pl.semaphore_wait(barrier, n - 1)
    point_copies = []
    for k in range(1, n_src):
        for i, (own, everyone) in enumerate([(own_shifts, shifts_ref), (own_weights, weights_ref)]):
            copy = pltpu.make_async_remote_copy(
                src_ref=own, dst_ref=everyone.at[src_id],
                send_sem=pt_send.at[i, k], recv_sem=pt_recv.at[i, k],
                device_id={"src": lax.rem(src_id + k, n_src)}, device_id_type=MESH,
            )
            copy.start()
            point_copies.append(copy)
    shifts_ref[src_id] = own_shifts[...]
    weights_ref[src_id] = own_weights[...]
    outgoing = []
    for k in range(1, n):
        other, where = partner(k)
        copy = pltpu.make_async_remote_copy(
            src_ref=send.at[pl.ds(pl.multiple_of(other * per, per), per)],
            dst_ref=arrived.at[k],
            send_sem=rs_send.at[k], recv_sem=rs_recv.at[k],
            device_id=where, device_id_type=MESH,
        )
        copy.start()
        outgoing.append(copy)
    for copy in point_copies:
        copy.wait_recv()
    to_scalars = [
        pltpu.make_async_copy(shifts_ref, shifts, point_sem.at[0]),
        pltpu.make_async_copy(weights_ref, weights, point_sem.at[1]),
    ]
    for copy in to_scalars:
        copy.start()
    for copy in to_scalars:
        copy.wait()
    sources, count = pupils.shape[0], weights.shape[2]
    along_rows = lax.broadcasted_iota(jnp.int32, (p, p), 1) - h
    along_cols = lax.broadcasted_iota(jnp.int32, (p, p), 0) - h
    radius = p // 4

    def make_pupil(s, carry):
        down = along_rows + shifts[s // count, 0, lax.rem(s, count)]
        across = along_cols + shifts[s // count, 1, lax.rem(s, count)]
        inside = down * down + across * across <= radius * radius
        pupils[s] = jnp.where(inside, 1.0, 0.0).astype(jnp.bfloat16)
        return carry

    lax.fori_loop(0, sources, make_pupil, 0)

    mine = pl.ds(pl.multiple_of(me * per, per), per)
    reduced = part[mine]
    for k, copy in enumerate(outgoing, 1):
        copy.wait_recv()
        reduced = reduced + arrived[k].astype(jnp.float32)
    spec_ref[mine] = reduced.astype(jnp.bfloat16)
    gathered = []
    for k in range(1, n):
        copy = pltpu.make_async_remote_copy(
            src_ref=spec_ref.at[mine], dst_ref=spec_ref.at[mine],
            send_sem=ag_send.at[k], recv_sem=ag_recv.at[k],
            device_id=partner(k)[1], device_id_type=MESH,
        )
        copy.start()
        gathered.append(copy)
    for copy in gathered:
        copy.wait_recv()
    for copy in outgoing + point_copies + gathered:
        copy.wait_send()

    for table in tables:
        table.wait()
    block = total.shape[1]
    lane = lax.broadcasted_iota(jnp.int32, (p, h), 1)
    line = lax.broadcasted_iota(jnp.int32, (p, h), 0)
    for i in range(2):
        kept = jnp.concatenate([spec_ref[:, i * p : (i + 1) * p], spec_ref[:, 2 * p :]], 1)
        picked = lax.dot_general(
            unfold_ref[i], kept, (((1,), (1,)), ((), ())), preferred_element_type=jnp.float32
        )
        holder = (i * p + line) // width * per
        middle = jnp.where(lane == holder, picked[2 * p :], 0.0)
        mirrored = jnp.concatenate([picked[p : 2 * p], middle], 1).astype(jnp.bfloat16)
        upper = jnp.dot(mirrored, back_ref[...], preferred_element_type=jnp.float32)
        turned[:, i * p : i * p + h] = picked[:p].astype(jnp.bfloat16)
        turned[:, i * p + h : (i + 1) * p] = upper.astype(jnp.bfloat16)

    def first(s, carry):
        pupil = pupils[s]
        passed = jnp.concatenate([turned[:, :p] * pupil, turned[:, p:] * pupil], 1)
        k = jnp.dot(passed, image_rows[...], preferred_element_type=jnp.float32).astype(jnp.bfloat16)
        halves[s, :p] = k
        halves[s, p:, :block] = -k[:, block:]
        halves[s, p:, block:] = k[:, :block]
        return carry

    lax.fori_loop(0, sources, first, 0, unroll=16)
    total[...] = jnp.zeros_like(total)

    def second(s, carry):
        weight = weights[s // count, 0, lax.rem(s, count)].astype(jnp.float32) * (1.0 / sources)
        e = jnp.dot(col_ref[...], halves[s], preferred_element_type=jnp.float32)
        total[...] += weight * (e[:, :block] * e[:, :block] + e[:, block:] * e[:, block:])
        return carry

    lax.fori_loop(0, sources, second, 0, unroll=16)


def spread_kernel(total, high_ref, low_ref, out_ref):
    summed = total[...].T
    top = summed.astype(jnp.bfloat16)
    rest = (summed - top.astype(jnp.float32)).astype(jnp.bfloat16)
    out_ref[...] = (
        jnp.dot(top, high_ref[...], preferred_element_type=jnp.float32)
        + jnp.dot(rest, high_ref[...], preferred_element_type=jnp.float32)
        + jnp.dot(top, low_ref[...], preferred_element_type=jnp.float32)
    )


def body(n_row, n_src, mask_clip, source_shifts, source_weights):
    n = n_row * n_src
    rows, cols = mask_clip.shape
    side = P_SIZE // 2
    kept = (side, 2 * P_SIZE + side)
    shifts, weights = source_shifts.T, source_weights[None, :]
    chunks = 8
    vmem = pl.BlockSpec(memory_space=pltpu.VMEM)
    hbm = pl.BlockSpec(memory_space=pltpu.HBM)
    unfold, back = unfold_tables(n)
    row_table, col_table, high, low = inverse_tables(n)
    block = NI // n
    count = source_weights.shape[0]
    sources = n_src * count
    total = pl.pallas_call(
        functools.partial(kernel, n_row, n_src, chunks),
        out_shape=jax.ShapeDtypeStruct((COARSE, block), jnp.float32),
        in_specs=[hbm] * 3 + [vmem] * 2 + [hbm] * 4,
        out_specs=vmem,
        scratch_shapes=[
            pltpu.VMEM((rows, cols), jnp.bfloat16),
            pltpu.VMEM((cols, 2 * P_SIZE), jnp.bfloat16),
            pltpu.VMEM((P_SIZE + 16, rows), jnp.bfloat16),
            pltpu.VMEM((rows, 2 * P_SIZE), jnp.bfloat16),
            pltpu.VMEM(kept, jnp.float32),
            pltpu.VMEM(kept, jnp.bfloat16),
            pltpu.VMEM((n, side // n, kept[1]), jnp.bfloat16),
            pltpu.VMEM(kept, jnp.bfloat16),
            pltpu.VMEM((n_src, 2, count), jnp.int32),
            pltpu.VMEM((n_src, 1, count), jnp.int32),
            pltpu.SMEM((n_src, 2, count), jnp.int32),
            pltpu.SMEM((n_src, 1, count), jnp.int32),
            pltpu.VMEM(unfold.shape, jnp.bfloat16),
            pltpu.VMEM(back.shape, jnp.bfloat16),
            pltpu.VMEM((2 * P_SIZE, 2 * block), jnp.bfloat16),
            pltpu.VMEM(col_table.shape, jnp.bfloat16),
            pltpu.VMEM((sources, P_SIZE, P_SIZE), jnp.bfloat16),
            pltpu.VMEM((P_SIZE, 2 * P_SIZE), jnp.bfloat16),
            pltpu.VMEM((sources, 2 * P_SIZE, 2 * block), jnp.bfloat16),
            pltpu.SemaphoreType.DMA((chunks + 2,)),
            pltpu.SemaphoreType.DMA((4,)),
            pltpu.SemaphoreType.DMA((2,)),
            pltpu.SemaphoreType.DMA((n,)),
            pltpu.SemaphoreType.DMA((n,)),
            pltpu.SemaphoreType.DMA((n,)),
            pltpu.SemaphoreType.DMA((n,)),
            pltpu.SemaphoreType.DMA((2, n_src)),
            pltpu.SemaphoreType.DMA((2, n_src)),
        ],
        compiler_params=pltpu.CompilerParams(
            collective_id=0, has_side_effects=True, vmem_limit_bytes=62 * 2**20
        ),
        name="image",
    )(
        mask_clip,
        jnp.asarray(forward_table(n_src * cols)),
        jnp.asarray(row_table_of(n_row * rows)),
        shifts,
        weights,
        *map(jnp.asarray, (unfold, back, row_table, col_table)),
    )
    return pl.pallas_call(
        spread_kernel,
        out_shape=jax.ShapeDtypeStruct((block, NI), jnp.float32),
        in_specs=[vmem] * 3,
        out_specs=vmem,
        compiler_params=pltpu.CompilerParams(vmem_limit_bytes=62 * 2**20),
        name="spread",
    )(total, jnp.asarray(high), jnp.asarray(low))


def solution(mesh):
    placed = (P(("clip", "row"), "src"), P("src", None), P("src"))
    return jax.shard_map(
        functools.partial(body, mesh.shape["row"], mesh.shape["src"]),
        mesh=mesh, in_specs=placed, out_specs=P(("clip", "row", "src"), None), check_vma=False,
    )
```
